128 devices in a mesh: src: 8 (over z_lo, y), tgt: 16 (over x, z_hi, core).
Axes of the slice: x: 4, y: 4, z: 4 (z_hi: 2, z_lo: 2; z = z_hi * 2 + z_lo), core: 2. Of those that a mesh axis runs over, the one named last changes fastest.
Arguments:
- source_values: float32 [16, 1048576], P(None, ('src', 'tgt')), may hold values from -6 to 6
- source_phase: float32 [1048576], P(('src', 'tgt')), may hold values from -3.140625 to 3.140625
- leaf_interp: bfloat16 [64, 64], replicated, may hold values from -0.75 to 0.75
- level_interp: bfloat16 [13, 2, 64, 64], replicated, may hold values from -0.5 to 0.5
- level_phase: float32 [13, 3, 16384, 64], P(None, None, ('src', 'tgt')), may hold values from -3.140625 to 3.140625
- middle_interp: bfloat16 [64, 64], replicated, may hold values from -0.75 to 0.75
- middle_phase: float32 [2, 16384, 64], P(None, ('src', 'tgt')), may hold values from -3.140625 to 3.140625
- final_phase: float32 [16384, 64], P(('src', 'tgt')), may hold values from -3.140625 to 3.140625
- final_interp: bfloat16 [64, 64], replicated, may hold values from -0.75 to 0.75
- target_phase: float32 [1048576], P(('src', 'tgt')), may hold values from -3.140625 to 3.140625
Outputs:
- target_values: float32 [2, 16, 1048576], P(None, None, ('src', 'tgt'))
The draws below stay inside these ranges and needn't reach their ends.
All inputs are finite; a program needn't handle non-finite values.
Results may differ from the reference program's by a relative error of at most 0.024.
Values may be sent and summed in bfloat16 or wider, within the bound.
No kernel may reach another device: no remote copies, remote signals or barrier semaphores. Data moves between devices by JAX's collectives and lax.ppermute only.
A program may use at most 64 MiB of HBM per device.

```python
import jax
import jax.numpy as jnp

RANK = 64
COLS = 128
RHS = 16
LEAF = 64
BLK_MUL = 1
LOCAL_SRC = 3
LOCAL_TGT = 3
LS = 3
LT = 4
NLEV = 13
BLK = 128
SLOTS = 16384
SOURCES = 1048576
N_SRC = 8
N_TGT = 16


def block_scale(key, shape, split, low, top_value):
    level = 1.0
    for axis_at, blocks in split:
        heights = jax.random.uniform(jax.random.fold_in(jax.random.fold_in(key, 6), axis_at), (blocks,), jnp.float32, low / len(split), top_value / len(split))
        level = level * jnp.repeat(jnp.exp(heights), shape[axis_at] // blocks).reshape((-1,) + (1,) * (len(shape) - 1 - axis_at))
    return level


def noise(rng, shape, scale, limit, split=(), dtype=jnp.bfloat16):
    factor_of = block_scale(rng, shape, split, -0.22, 0.18) if split else 1.0
    values = jax.random.normal(rng, shape, jnp.float32) * scale * factor_of
    return jnp.minimum(jnp.maximum(values, -limit), limit).astype(dtype)


def setup_inputs(seed: int = 0) -> dict:
    splits = jax.random.split(jax.random.key(seed), 11)
    source_values = noise(splits[0], (RHS, SOURCES), 1.0, 6.0, ((1, 128),), jnp.float32)
    source_phase = jnp.clip(jax.random.uniform(splits[1], (SOURCES,), jnp.float32, -3.140625, 3.140625), -3.140625, 3.140625)
    leaf_interp = noise(splits[2], (LEAF, RANK), LEAF ** -0.5, 0.75)
    level_interp = noise(splits[3], (NLEV, 2, RANK, RANK), (2 * RANK) ** -0.5, 0.5)
    level_phase = jnp.clip(jax.random.uniform(splits[4], (NLEV, 3, SLOTS, RANK), jnp.float32, -3.140625, 3.140625), -3.140625, 3.140625)
    middle_interp = noise(splits[5], (RANK, RANK), RANK ** -0.5, 0.75)
    middle_phase = jnp.clip(jax.random.uniform(splits[6], (2, SLOTS, RANK), jnp.float32, -3.140625, 3.140625), -3.140625, 3.140625)
    final_phase = jnp.clip(jax.random.uniform(splits[7], (SLOTS, RANK), jnp.float32, -3.140625, 3.140625), -3.140625, 3.140625)
    final_interp = noise(splits[8], (RANK, LEAF), RANK ** -0.5, 0.75)
    target_phase = jnp.clip(jax.random.uniform(splits[9], (SOURCES,), jnp.float32, -3.140625, 3.140625), -3.140625, 3.140625)
    return {"source_values": source_values, "source_phase": source_phase, "leaf_interp": leaf_interp, "level_interp": level_interp, "level_phase": level_phase, "middle_interp": middle_interp, "middle_phase": middle_phase, "final_phase": final_phase, "final_interp": final_interp, "target_phase": target_phase}


def rotate(vectors, angles):
    half_width = angles.shape[-1]
    values = vectors.astype(jnp.float32)
    real_part = values[..., :half_width]
    imag_part = values[..., half_width:]
    cosine = jnp.cos(angles)[:, None, :]
    sine_val = jnp.sin(angles)[:, None, :]
    return jnp.concatenate([real_part * cosine - imag_part * sine_val, real_part * sine_val + imag_part * cosine], -1)


def block_pair(matrix):
    zeros_block = jnp.zeros_like(matrix)
    upper_rows = jnp.concatenate([matrix, zeros_block], 1)
    lower_rows = jnp.concatenate([zeros_block, matrix], 1)
    return jnp.concatenate([upper_rows, lower_rows], 0)


def flip_pairs(coeffs, stride):
    shape = coeffs.shape
    return coeffs.reshape((shape[0] // (2 * stride), 2, stride) + shape[1:])[:, ::-1].reshape(shape)


def translate(coeffs, partner, phases, matrices):
    shape = coeffs.shape
    own_rot = rotate(coeffs, phases[0]).astype(jnp.bfloat16).reshape(-1, shape[2])
    other_rot = rotate(partner, phases[1]).astype(jnp.bfloat16).reshape(-1, shape[2])
    summed = jnp.dot(own_rot, block_pair(matrices[0]), preferred_element_type=jnp.float32)
    summed = summed + jnp.dot(other_rot, block_pair(matrices[1]), preferred_element_type=jnp.float32)
    return rotate(summed.reshape(shape), phases[2]).astype(jnp.bfloat16)


def reference(source_values, source_phase, leaf_interp, level_interp, level_phase, middle_interp, middle_phase, final_phase, final_interp, target_phase):
    cos_src = jnp.cos(source_phase)[None, :]
    sin_src = jnp.sin(source_phase)[None, :]
    modulated = jnp.stack([source_values * cos_src, -source_values * sin_src]).astype(jnp.bfloat16)
    leaf_terms = jnp.dot(modulated.reshape(-1, LEAF), leaf_interp, preferred_element_type=jnp.float32)
    leaf_terms = leaf_terms.reshape(2, RHS, SLOTS, RANK).transpose(2, 1, 0, 3)
    coeffs = leaf_terms.reshape(SLOTS, RHS, COLS).astype(jnp.bfloat16)
    level_index = 0
    for step_index in range(LOCAL_SRC):
        partner = flip_pairs(coeffs, 2 ** step_index)
        coeffs = translate(coeffs, partner, level_phase[level_index], level_interp[level_index])
        level_index += 1
    for step_index in range(LS):
        partner = flip_pairs(coeffs, (SLOTS // N_SRC) * 2 ** step_index)
        coeffs = translate(coeffs, partner, level_phase[level_index], level_interp[level_index])
        level_index += 1
    devices = N_SRC * N_TGT
    regrouped = coeffs.reshape(devices, devices, BLK_MUL, RHS, COLS).transpose(1, 0, 2, 3, 4).reshape(SLOTS, RHS, COLS)
    switched = rotate(regrouped, middle_phase[0]).astype(jnp.bfloat16).reshape(-1, COLS)
    middle_sum = jnp.dot(switched, block_pair(middle_interp), preferred_element_type=jnp.float32)
    coeffs = rotate(middle_sum.reshape(SLOTS, RHS, COLS), middle_phase[1]).astype(jnp.bfloat16)
    for step_index in range(LT):
        partner = flip_pairs(coeffs, BLK * 2 ** step_index)
        coeffs = translate(coeffs, partner, level_phase[level_index], level_interp[level_index])
        level_index += 1
    for step_index in range(LOCAL_TGT):
        partner = flip_pairs(coeffs, 2 ** step_index)
        coeffs = translate(coeffs, partner, level_phase[level_index], level_interp[level_index])
        level_index += 1
    finals = rotate(coeffs, final_phase).astype(jnp.bfloat16)
    finals = finals.reshape(SLOTS, RHS, 2, RANK).transpose(2, 1, 0, 3).reshape(-1, RANK)
    evaluated = jnp.dot(finals, final_interp, preferred_element_type=jnp.float32).reshape(2, RHS, SOURCES)
    cos_tgt = jnp.cos(target_phase)[None, :]
    sin_tgt = jnp.sin(target_phase)[None, :]
    real_out = evaluated[0] * cos_tgt - evaluated[1] * sin_tgt
    imag_out = evaluated[0] * sin_tgt + evaluated[1] * cos_tgt
    return jnp.stack([real_out, imag_out])
```

```python
import functools

import jax
import jax.numpy as jnp
from jax import lax
from jax.experimental import pallas as pl
from jax.experimental.pallas import tpu as pltpu
from jax.sharding import PartitionSpec as P

F32 = jnp.float32
BF16 = jnp.bfloat16
CHUNK = 32
SIN_FIT = (3.14159258, -5.16770688, 2.55003138, -0.59804517, 0.07722012)
COS_FIT = (0.99999995, -4.93479286, 4.05841191, -1.33188014, 0.21969675)


def cos_sin(theta):
    turns = theta * F32(0.15915494309189535)
    turns = turns - jnp.round(turns)
    square = turns * turns
    sin_half = F32(SIN_FIT[4])
    cos_half = F32(COS_FIT[4])
    for k in (3, 2, 1, 0):
        sin_half = sin_half * square + F32(SIN_FIT[k])
        cos_half = cos_half * square + F32(COS_FIT[k])
    sin_half = sin_half * turns
    twice = sin_half + sin_half
    return 1.0 - twice * sin_half, twice * cos_half


def iota(shape, axis):
    return lax.broadcasted_iota(jnp.int32, shape, axis)


def xor_partner(values, stride, axis):
    size = values.shape[axis]
    bit = (iota(values.shape, axis) & stride) != 0
    return jnp.where(
        bit, pltpu.roll(values, stride, axis), pltpu.roll(values, size - stride, axis)
    )


def permutation(row_of):
    rows = iota((128, 128), 0)
    columns = iota((128, 128), 1)
    return jnp.where(columns == row_of(rows), 1.0, 0.0).astype(BF16)


def dot_last(left, right):
    return lax.dot_general(left, right, (((1,), (1,)), ((), ())), preferred_element_type=F32)


def swap_digits(rows):
    return (rows & 7) * 16 + (rows >> 3)


def swap_digits_back(rows):
    return (rows & 15) * 8 + (rows >> 4)


def halves(matrix):
    doubled = jnp.concatenate([matrix, matrix], 1)
    low = iota(doubled.shape, 1) < 64
    zeros = jnp.zeros_like(doubled)
    return jnp.where(low, doubled, zeros), jnp.where(low, zeros, doubled)


def put_weights(weights, matrices):
    at = 0
    for matrix in matrices:
        low, high = halves(matrix.astype(F32))
        for block in (low, high, high, -low):
            weights[at : at + 64, :] = block.astype(BF16)
            at += 64


def transposed_trig(angles, perm, table):
    rows = []
    for theta in angles:
        cosine, sine = cos_sin(theta)
        cosine = cosine.astype(BF16)
        sine = sine.astype(BF16)
        rows += [cosine, cosine, sine, sine]
    stacked = jnp.concatenate(rows, 0)
    width = 256 * len(angles)
    table[:, :, 0:width] = dot_last(perm, stacked).reshape(16, 8, width)


def row_trig(theta, table):
    cosine, sine = cos_sin(theta)
    low = iota(theta.shape, 1) < 64
    for at, value in ((0, cosine), (128, sine)):
        turned = pltpu.roll(value, 64, 1)
        own = jnp.where(low, value, turned)
        other = jnp.where(low, turned, value)
        table[:, :, at : at + 128] = own.reshape(16, 8, 128)
        table[:, :, at + 256 : at + 384] = other.reshape(16, 8, 128)


def apply_stage(load, table, weights, left, store, stride):
    width = 256 if stride is None else 512

    def chunk(step, carry):
        base = pl.multiple_of(step * CHUNK, CHUNK)
        for i in range(CHUNK):
            own = load(base + i)
            group = step * (CHUNK // 8) + i // 8
            row = slice(i % 8, i % 8 + 1)
            span = slice(16 * i, 16 * i + 16)
            parts = [own, own]
            if stride is not None:
                other = load((base ^ (stride & ~(CHUNK - 1))) + (i ^ (stride & (CHUNK - 1))))
                parts += [other, other]
            for q, part in enumerate(parts):
                factor = jnp.broadcast_to(
                    table[group, row, 128 * q : 128 * q + 128], (16, 128)
                )
                left[span, 128 * q : 128 * q + 128] = part * factor.astype(BF16)
        product = jnp.dot(
            left[:, :width], weights[:width, :], preferred_element_type=F32
        ).astype(BF16)
        for i in range(CHUNK):
            store(base + i, product[16 * i : 16 * i + 16])
        return carry

    lax.fori_loop(0, 128 // CHUNK, chunk, 0)


def loader(ref):
    return lambda slot: ref[slot]


def storer(ref):
    def store(slot, value):
        ref[slot] = value

    return store


def angle_kernel(low_levels, high_levels, middle, out):
    pieces = [middle[0], middle[1]]
    for ref, n in ((low_levels, 0), (low_levels, 1), (high_levels, 0), (high_levels, 1)):
        pieces += [ref[n, 0], ref[n, 1]]
    pieces += [low_levels[0, 2], low_levels[1, 2], high_levels[0, 2], high_levels[0, 2]]
    stacked = jnp.concatenate([piece.astype(BF16) for piece in pieces], 0)
    out[...] = dot_last(permutation(swap_digits), stacked).astype(BF16)


def source_kernel(values, phase, phases, leaf, interp, out, coeffs, spare, table, left, weights):
    slots = lambda rows: rows
    perm = permutation(slots)
    pieces = [phases[n, q] for n in (3, 4, 5) for q in (0, 1)]
    pieces += [phases[n, 2] for n in (2, 3, 4, 5)]
    stacked = jnp.concatenate([piece.astype(BF16) for piece in pieces], 0)
    sent = dot_last(perm, stacked).astype(BF16)
    for e in range(8):
        for p in range(5):
            out[e, 16 + p] = sent[16 * e : 16 * e + 16, 128 * p : 128 * p + 128]
    cosine, sine = cos_sin(phase[...])
    table[0:8, :, 0:128] = cosine.reshape(8, 8, 128)
    table[0:8, :, 128:256] = sine.reshape(8, 8, 128)
    low, high = halves(leaf[...].astype(F32))
    zeros = jnp.zeros_like(low)
    for at, first, second in ((0, low, zeros), (64, zeros, low), (128, high, zeros), (192, zeros, high)):
        weights[at : at + 64, :] = first.astype(BF16)
        weights[256 + at : 256 + at + 64, :] = second.astype(BF16)
    pairs = CHUNK
    for step in range(64 // pairs):
        for i in range(pairs):
            pair = step * pairs + i
            block = values[:, 128 * pair : 128 * pair + 128]
            span = slice(16 * i, 16 * i + 16)
            left[span, 0:128] = (block * table[pair >> 3, pair & 7 : (pair & 7) + 1, 0:128]).astype(BF16)
            left[span, 128:256] = (-block * table[pair >> 3, pair & 7 : (pair & 7) + 1, 128:256]).astype(BF16)
        for odd in range(2):
            product = jnp.dot(
                left[:, :256], weights[256 * odd : 256 * odd + 256, :], preferred_element_type=F32
            ).astype(BF16)
            for i in range(pairs):
                coeffs[2 * (step * pairs + i) + odd] = product[16 * i : 16 * i + 16]

    def send(slot, value):
        out[slot >> 4, slot & 15] = value

    for n, source, store in (
        (0, coeffs, storer(spare)),
        (1, spare, storer(coeffs)),
        (2, coeffs, send),
    ):
        own, other = phases[n, 0], phases[n, 1]
        if n:
            own = own + phases[n - 1, 2]
            other = other + xor_partner(phases[n - 1, 2], 2**n, 1)
        transposed_trig([own, other], perm, table)
        put_weights(weights, [interp[n, 0], interp[n, 1]])
        apply_stage(loader(source), table, weights, left, store, 2**n)


def middle_kernel(received, angles, interp, middle_interp, out, coeffs, spare, table, left, weights):
    low = iota((128, 128), 1) < 64

    def both(value, half):
        turned = pltpu.roll(value, 64, 1)
        return jnp.where(low, value, turned) if half == 0 else jnp.where(low, turned, value)

    def with_partner(value, stride):
        return jnp.where(low, value, xor_partner(value, stride, 0))

    perm = permutation(swap_digits)
    early = []
    for p in range(5):
        piece = jnp.concatenate([received[d, 16 + p] for d in range(8)], 0)
        early.append(jnp.dot(perm, piece, preferred_element_type=F32))
    late = lambda p: angles[:, 128 * p : 128 * p + 128].astype(F32)

    def arrived(slot):
        return received[slot & 7, slot >> 3]

    def send(slot, value):
        out[slot] = value

    first = loader(coeffs)
    second = loader(spare)
    pending = both(early[3], 0)
    for j, (load, store) in enumerate(
        ((arrived, storer(coeffs)), (first, storer(spare)), (second, storer(coeffs)))
    ):
        row_trig(early[j] + with_partner(pending, 2**j), table)
        put_weights(weights, [interp[3 + j, 0], interp[3 + j, 1]])
        apply_stage(load, table, weights, left, store, 2**j)
        pending = both(early[3 + (j + 1) // 2], (j + 1) % 2)
    cosine, sine = cos_sin(pending + both(late(0), 0))
    table[:, :, 0:128] = cosine.reshape(16, 8, 128)
    table[:, :, 128:256] = sine.reshape(16, 8, 128)
    put_weights(weights, [middle_interp[...]])
    apply_stage(first, table, weights, left, storer(spare), None)
    pending = both(late(0), 1)
    for j, (load, store) in enumerate(
        (
            (second, storer(coeffs)),
            (first, storer(spare)),
            (second, storer(coeffs)),
            (first, send),
        )
    ):
        row_trig(late(1 + j) + with_partner(pending, 8 * 2**j), table)
        put_weights(weights, [interp[6 + j, 0], interp[6 + j, 1]])
        apply_stage(load, table, weights, left, store, 8 * 2**j)
        if j < 3:
            pending = both(late(5 + j // 2), j % 2)


def target_kernel(
    received, before, phases10, phases11, phases12, final, interp, final_interp, phase, out,
    coeffs, spare, table, left, weights, trig, final_weights,
):
    perm = permutation(swap_digits)
    pending = before[0, 2]
    for j, (ref, load, store) in enumerate(
        (
            (phases10, loader(received), storer(coeffs)),
            (phases11, loader(coeffs), storer(spare)),
            (phases12, loader(spare), storer(coeffs)),
        )
    ):
        own = ref[0, 0] + pending
        other = ref[0, 1] + xor_partner(pending, 2**j, 1)
        transposed_trig([own, other], perm, table)
        put_weights(weights, [interp[10 + j, 0], interp[10 + j, 1]])
        apply_stage(load, table, weights, left, store, 8 * 2**j)
        pending = ref[0, 2]
    transposed_trig([final[...] + pending], perm, table)
    cosine, sine = cos_sin(phase[...])
    trig[:, 0:128] = cosine
    trig[:, 128:256] = sine
    low, high = halves(final_interp[...].astype(F32))
    zeros = jnp.zeros_like(low)
    at = 0
    for block in (low, high):
        for real, imag in ((block, zeros), (zeros, block), (zeros, block), (-block, zeros)):
            final_weights[at : at + 64, 0:128] = real.astype(BF16)
            final_weights[at : at + 64, 128:256] = imag.astype(BF16)
            at += 64
    pairs = CHUNK
    for step in range(64 // pairs):
        for i in range(pairs):
            pair = step * pairs + i
            even = (2 * (pair & 7)) * 8 + (pair >> 3)
            span = slice(16 * i, 16 * i + 16)
            for q, slot in enumerate((even, even + 8)):
                value = coeffs[slot]
                for half in range(2):
                    row = table[
                        slot >> 3, slot & 7 : (slot & 7) + 1, 128 * half : 128 * half + 128
                    ]
                    factor = jnp.broadcast_to(row, (16, 128)).astype(BF16)
                    left[span, 256 * q + 128 * half : 256 * q + 128 * half + 128] = value * factor
        product = jnp.dot(left[...], final_weights[...], preferred_element_type=F32)
        for i in range(pairs):
            pair = step * pairs + i
            real = product[16 * i : 16 * i + 16, 0:128]
            imag = product[16 * i : 16 * i + 16, 128:256]
            cosine = trig[pair : pair + 1, 0:128]
            sine = trig[pair : pair + 1, 128:256]
            out[0, :, 128 * pair : 128 * pair + 128] = real * cosine - imag * sine
            out[1, :, 128 * pair : 128 * pair + 128] = real * sine + imag * cosine


def whole(shape):
    return pl.BlockSpec(shape, lambda i: (0,) * len(shape))


def levels(count, index):
    return pl.BlockSpec((count, 3, 64, 128), lambda i: (index, 0, 0, 0))


def scratch():
    return [
        pltpu.VMEM((128, 16, 128), BF16),
        pltpu.VMEM((128, 16, 128), BF16),
        pltpu.VMEM((16, 8, 512), F32),
        pltpu.VMEM((CHUNK * 16, 512), BF16),
        pltpu.VMEM((512, 128), BF16),
    ]


PARAMS = pltpu.CompilerParams(vmem_limit_bytes=40 * 1024 * 1024)


def shards(
    source_values,
    source_phase,
    leaf_interp,
    level_interp,
    level_phase,
    middle_interp,
    middle_phase,
    final_phase,
    final_interp,
    target_phase,
):
    phases = jnp.swapaxes(level_phase, 2, 3)
    middle = jnp.swapaxes(middle_phase, 1, 2)
    final = jnp.swapaxes(final_phase, 0, 1)
    angles = pl.pallas_call(
        angle_kernel,
        grid=(1,),
        in_specs=[levels(2, 3), levels(2, 4), whole((2, 64, 128))],
        out_specs=whole((128, 896)),
        out_shape=jax.ShapeDtypeStruct((128, 896), BF16),
        compiler_params=PARAMS,
        name="angles",
    )(phases, phases, middle)
    angles = lax.all_to_all(
        angles.reshape(16, 8, 896), "tgt", split_axis=0, concat_axis=0, tiled=True
    ).reshape(128, 896)
    sent = pl.pallas_call(
        source_kernel,
        grid=(1,),
        in_specs=[
            whole((16, 8192)),
            whole((64, 128)),
            levels(6, 0),
            whole((64, 64)),
            whole((13, 2, 64, 64)),
        ],
        out_specs=whole((8, 21, 16, 128)),
        out_shape=jax.ShapeDtypeStruct((8, 21, 16, 128), BF16),
        scratch_shapes=scratch(),
        compiler_params=PARAMS,
        name="source_side",
    )(source_values, source_phase.reshape(64, 128), phases, leaf_interp, level_interp)
    received = lax.all_to_all(sent, "src", split_axis=0, concat_axis=0, tiled=True)
    sent = pl.pallas_call(
        middle_kernel,
        grid=(1,),
        in_specs=[
            whole((8, 21, 16, 128)),
            whole((128, 896)),
            whole((13, 2, 64, 64)),
            whole((64, 64)),
        ],
        out_specs=whole((128, 16, 128)),
        out_shape=jax.ShapeDtypeStruct((128, 16, 128), BF16),
        scratch_shapes=scratch(),
        compiler_params=PARAMS,
        name="middle",
    )(received, angles, level_interp, middle_interp)
    received = lax.all_to_all(sent, "tgt", split_axis=0, concat_axis=0, tiled=True)
    return pl.pallas_call(
        target_kernel,
        grid=(1,),
        in_specs=[
            whole((128, 16, 128)),
            levels(1, 9),
            levels(1, 10),
            levels(1, 11),
            levels(1, 12),
            whole((64, 128)),
            whole((13, 2, 64, 64)),
            whole((64, 64)),
            whole((64, 128)),
        ],
        out_specs=whole((2, 16, 8192)),
        out_shape=jax.ShapeDtypeStruct((2, 16, 8192), F32),
        scratch_shapes=scratch()
        + [pltpu.VMEM((64, 256), F32), pltpu.VMEM((512, 256), BF16)],
        compiler_params=PARAMS,
        name="target_side",
    )(
        received,
        phases,
        phases,
        phases,
        phases,
        final,
        level_interp,
        final_interp,
        target_phase.reshape(64, 128),
    )


def solution(mesh):
    return jax.shard_map(
        shards,
        mesh=mesh,
        in_specs=(
            P(None, ("src", "tgt")),
            P(("src", "tgt")),
            P(),
            P(),
            P(None, None, ("src", "tgt"), None),
            P(),
            P(None, ("src", "tgt"), None),
            P(("src", "tgt"), None),
            P(),
            P(("src", "tgt")),
        ),
        out_specs=P(None, None, ("src", "tgt")),
        check_vma=False,
    )
```

```python
import functools

import functools

import jax
import jax.numpy as jnp
from jax import lax
from jax.experimental import pallas as pl
from jax.experimental.pallas import tpu as pltpu
from jax.sharding import PartitionSpec as P

F32 = jnp.float32
BF16 = jnp.bfloat16
PAIRS = 16
E_PARTS = ((0, 1),)
D_PARTS = ((0, 1),)
SIN_FIT = (3.14159258, -5.16770688, 2.55003138, -0.59804517, 0.07722012)
COS_FIT = (0.99999995, -4.93479286, 4.05841191, -1.33188014, 0.21969675)


def cos_sin(theta):
    turns = theta * F32(0.15915494309189535)
    turns = turns - jnp.round(turns)
    square = turns * turns
    sin_half = F32(SIN_FIT[4])
    cos_half = F32(COS_FIT[4])
    for k in (3, 2, 1, 0):
        sin_half = sin_half * square + F32(SIN_FIT[k])
        cos_half = cos_half * square + F32(COS_FIT[k])
    sin_half = sin_half * turns
    twice = sin_half + sin_half
    return 1.0 - twice * sin_half, twice * cos_half


def iota(shape, axis):
    return lax.broadcasted_iota(jnp.int32, shape, axis)


def xor_partner(values, stride, axis):
    size = values.shape[axis]
    bit = (iota(values.shape, axis) & stride) != 0
    return jnp.where(
        bit, pltpu.roll(values, stride, axis), pltpu.roll(values, size - stride, axis)
    )


def dot_last(left, right):
    return lax.dot_general(left, right, (((1,), (1,)), ((), ())), preferred_element_type=F32)


def permutation(size, row_of):
    rows = iota((size, size), 0)
    columns = iota((size, size), 1)
    return jnp.where(columns == row_of(rows), 1.0, 0.0).astype(BF16)


def lower(shape):
    return iota(shape, 1) < 64


def halves(matrix):
    matrix = matrix.astype(F32)
    doubled = jnp.concatenate([matrix, matrix], 1)
    zeros = jnp.zeros_like(doubled)
    low = lower(doubled.shape)
    return (
        jnp.where(low, doubled, zeros).astype(BF16),
        jnp.where(low, zeros, doubled).astype(BF16),
        zeros.astype(BF16),
    )


def put_weights(weights, matrices):
    for n, matrix in enumerate(matrices):
        low, high, _ = halves(matrix)
        weights[128 * n : 128 * n + 64, :] = low
        weights[128 * n + 64 : 128 * n + 128, :] = high


def put_trig(theta, table):
    low = lower(theta.shape)
    for at, value in zip((0, 128), cos_sin(theta)):
        turned = pltpu.roll(value, 64, 1)
        table[:, at : at + 128] = jnp.where(low, value, turned)
        table[:, at + 256 : at + 384] = jnp.where(low, turned, value)


def put_single_trig(theta, table):
    cosine, sine = cos_sin(theta)
    table[:, 0:128] = cosine
    table[:, 128:256] = sine


def turn(table, row, at, tile):
    real, imag = tile
    cosine = table[row : row + 1, at : at + 128]
    sine = table[row : row + 1, at + 128 : at + 256]
    turned = jnp.concatenate([real * cosine - imag * sine, real * sine + imag * cosine], 0)
    return turned.astype(BF16)


def split(tile):
    tile = tile.astype(F32)
    return tile[0:8], tile[8:16]


def level(pairs, load, row_of, table, weights, left, store):
    for step in range(0, len(pairs), PAIRS):
        rows = left.at[(step // PAIRS) % 2]
        chunk = pairs[step : step + PAIRS]
        slots = []
        for pair in chunk:
            tiles = [split(load(slot)) for slot in pair]
            for slot, own, other in zip(pair, tiles, tiles[::-1]):
                span = slice(16 * len(slots), 16 * len(slots) + 16)
                rows[span, 0:128] = turn(table, row_of(slot), 0, own)
                rows[span, 128:256] = turn(table, row_of(slot), 256, other)
                slots.append(slot)
        size = 16 * len(slots)
        product = jnp.dot(rows[:size, :], weights[...], preferred_element_type=F32).astype(BF16)
        for i, slot in enumerate(slots):
            store(slot, product[16 * i : 16 * i + 16])


def pairs_of(slots, partner):
    return [(slot, partner(slot)) for slot in slots if slot < partner(slot)]


def storer(ref):
    def store(slot, value):
        ref[slot] = value

    return store


def loader(ref):
    return lambda slot: ref[slot]


def angle_kernel(low_levels, high_levels, middle, out):
    pieces = [middle[0], middle[1]]
    for ref, n in ((low_levels, 0), (low_levels, 1), (high_levels, 0), (high_levels, 1)):
        pieces += [ref[n, 0], ref[n, 1]]
    pieces += [low_levels[0, 2], low_levels[1, 2], high_levels[0, 2], high_levels[0, 2]]
    stacked = jnp.concatenate([piece.astype(BF16) for piece in pieces], 0)
    perm = permutation(128, lambda rows: (rows & 7) * 16 + (rows >> 3))
    out[...] = dot_last(perm, stacked).astype(BF16)


def source_kernel(
    part, values, phase, phases, leaf, interp, out, coeffs, spare, tables, left, weights, trig, wide
):
    count = 8 * len(part)

    def rows_here(value):
        if len(part) == 2:
            return value
        width = value.shape[1]
        return value.reshape(8, 2, 8, width)[:, part[0]].reshape(64, width)

    pieces = [phases[n, q] for n in (3, 4, 5) for q in (0, 1)]
    pieces += [phases[n, 2] for n in (2, 3, 4, 5)]
    stacked = jnp.concatenate([piece.astype(BF16) for piece in pieces], 0)
    sent = rows_here(dot_last(permutation(128, lambda rows: rows), stacked))
    for e in range(8):
        here = sent[count * e : count * e + count]
        if len(part) == 2:
            for p in range(5):
                out[e, count + p] = here[:, 128 * p : 128 * p + 128].astype(BF16)
        else:
            for p in range(3):
                first = here[:, 256 * p : 256 * p + 128]
                second = here[:, 256 * p + 128 : 256 * p + 256] if p < 2 else first
                out[e, count + p] = jnp.concatenate([first, second], 0).astype(BF16)
    for n in range(3):
        own, other = phases[n, 0], phases[n, 1]
        if n:
            own = own + phases[n - 1, 2]
            other = other + xor_partner(phases[n - 1, 2], 2**n, 1)
        put_trig(rows_here(jnp.transpose(jnp.concatenate([own, other], 0))), tables.at[n])
        put_weights(weights.at[n], [interp[n, 0], interp[n, 1]])
    put_single_trig(phase[...], trig)
    low, high, zeros = halves(leaf[...])
    for n, first, second in ((0, low, zeros), (1, zeros, low), (2, high, zeros), (3, zeros, high)):
        wide[64 * n : 64 * n + 64, 0:128] = first
        wide[64 * n : 64 * n + 64, 128:256] = second
    leaf_pairs = [pair for pair in range(64) if (pair >> 2) & 1 in part]
    place = lambda slot: (slot >> 4) * count + (slot & (count - 1))
    for step in range(0, len(leaf_pairs), 32):
        rows = left.at[(step // 32) % 2]
        chunk = leaf_pairs[step : step + 32]
        for i, pair in enumerate(chunk):
            cosine = trig[pair : pair + 1, 0:128]
            sine = -trig[pair : pair + 1, 128:256]
            for half in range(2):
                block = values[8 * half : 8 * half + 8, 128 * pair : 128 * pair + 128]
                tile = jnp.concatenate([block * cosine, block * sine], 0).astype(BF16)
                rows[16 * i : 16 * i + 16, 128 * half : 128 * half + 128] = tile
        product = jnp.dot(rows[...], wide[...], preferred_element_type=F32).astype(BF16)
        for i, pair in enumerate(chunk):
            coeffs[place(2 * pair)] = product[16 * i : 16 * i + 16, 0:128]
            coeffs[place(2 * pair + 1)] = product[16 * i : 16 * i + 16, 128:256]

    def send(slot, value):
        out[slot // count, slot % count] = value

    slots = range(8 * count)
    for n, load, store in (
        (0, loader(coeffs), storer(spare)),
        (1, loader(spare), storer(coeffs)),
        (2, loader(coeffs), send),
    ):
        pairs = pairs_of(slots, lambda slot: slot ^ 2**n)
        level(pairs, load, lambda slot: slot, tables.at[n], weights.at[n], left, store)


def both(value, half):
    low = lower(value.shape)
    turned = pltpu.roll(value, 64, 1)
    return jnp.where(low, value, turned) if half == 0 else jnp.where(low, turned, value)


def with_partner(value, stride):
    return jnp.where(lower(value.shape), value, xor_partner(value, stride, 0))


def middle_kernel(
    part, received, angles, interp, middle_interp, out, coeffs, spare, tables, left, weights
):
    count = 8 * len(part)
    size = 8 * count
    early = []
    for p in range(5):
        if len(part) == 2:
            tiles = [received[d, count + p].astype(F32) for d in range(8)]
        else:
            at = 8 * (p % 2)
            tiles = [received[d, count + p // 2].astype(F32)[at : at + 8] for d in range(8)]
        early.append(jnp.concatenate(tiles, 0))
    late = lambda p: angles[:, 128 * p : 128 * p + 128].astype(F32)
    pending = both(early[3], 0)
    for j in range(3):
        put_trig(early[j] + with_partner(pending, count * 2**j), tables.at[j])
        put_weights(weights.at[j], [interp[3 + j, 0], interp[3 + j, 1]])
        pending = both(early[3 + (j + 1) // 2], (j + 1) % 2)
    perm = permutation(size, lambda rows: (rows & 7) * count + (rows >> 3))
    pending = jnp.dot(perm, pending.astype(BF16), preferred_element_type=F32)
    put_single_trig(pending + both(late(0), 0), tables.at[3])
    put_weights(weights.at[3], [middle_interp[...]])
    pending = both(late(0), 1)
    for j in range(len(part) + 2):
        put_trig(late(1 + j) + with_partner(pending, 8 * 2**j), tables.at[4 + j])
        put_weights(weights.at[4 + j], [interp[6 + j, 0], interp[6 + j, 1]])
        if j < 3:
            pending = both(late(5 + j // 2), j % 2)

    def arrived(slot):
        return received[slot & 7, slot >> 3]

    def turned_row(slot):
        return (slot & 7) * count + (slot >> 3)

    slots = range(size)
    stores = [storer(coeffs), storer(spare)]
    loads = [loader(coeffs), loader(spare)]
    for j in range(3):
        level(
            pairs_of(slots, lambda slot: slot ^ 2**j),
            arrived if j == 0 else loads[(j + 1) % 2],
            turned_row,
            tables.at[j],
            weights.at[j],
            left,
            stores[j % 2],
        )
    for step in range(0, size, 32):
        rows = left.at[(step // 32) % 2]
        for i in range(32):
            tile = split(coeffs[step + i])
            rows[16 * i : 16 * i + 16, 0:128] = turn(tables.at[3], step + i, 0, tile)
        product = jnp.dot(
            rows[:, 0:128], weights[3, 0:128, :], preferred_element_type=F32
        ).astype(BF16)
        for i in range(32):
            spare[step + i] = product[16 * i : 16 * i + 16]
    last = len(part) + 1
    for j in range(last + 1):
        level(
            pairs_of(slots, lambda slot: slot ^ 8 * 2**j),
            loads[(j + 1) % 2],
            lambda slot: slot,
            tables.at[4 + j],
            weights.at[4 + j],
            left,
            storer(out) if j == last else stores[j % 2],
        )


def join_kernel(first, second, angles, interp, *rest):
    outs = rest[: len(D_PARTS)]
    tables, left, weights = rest[len(D_PARTS) :]
    pending = both(angles[:, 768:896].astype(F32), 0)
    theta = angles[:, 512:640].astype(F32) + with_partner(pending, 64)
    put_trig(theta, tables)
    put_weights(weights, [interp[9, 0], interp[9, 1]])
    for part, out in zip(D_PARTS, outs):
        each = 4 * len(part)

        def load(slot):
            return first[slot] if slot < 64 else second[slot - 64]

        def send(slot, value):
            out[slot >> 3, slot & (each - 1)] = value

        slots = [slot for slot in range(128) if (slot >> 2) & 1 in part]
        pairs = pairs_of(slots, lambda slot: slot ^ 64)
        level(pairs, load, lambda slot: slot, tables, weights, left, send)


def target_kernel(
    part, received, before, phases10, phases11, phases12, final, interp, final_interp, phase, *rest
):
    out, coeffs, spare, tables, left, weights, trig, wide = rest[-8:]
    each = 4 * len(part)
    size = 16 * each
    first_row = 64 * part[0]

    def rows_here(value):
        return value[first_row : first_row + size]

    pending = before[0, 2]
    for j, ref in enumerate((phases10, phases11, phases12)):
        own = ref[0, 0] + pending
        other = ref[0, 1] + xor_partner(pending, 2**j, 1)
        put_trig(rows_here(jnp.transpose(jnp.concatenate([own, other], 0))), tables.at[j])
        put_weights(weights.at[j], [interp[10 + j, 0], interp[10 + j, 1]])
        pending = ref[0, 2]
    pending = final[...] + pending
    put_single_trig(
        rows_here(jnp.transpose(jnp.concatenate([pending, pending], 0))), tables.at[3]
    )
    put_single_trig(phase[...], trig)
    low, high, zeros = halves(final_interp[...])
    for n, first, second in ((0, low, zeros), (1, zeros, low), (2, high, zeros), (3, zeros, high)):
        wide[64 * n : 64 * n + 64, 0:128] = first
        wide[64 * n : 64 * n + 64, 128:256] = second
    slots = range(size)
    for j, load, store in (
        (0, lambda slot: received[slot & 15, slot >> 4], storer(coeffs)),
        (1, loader(coeffs), storer(spare)),
        (2, loader(spare), storer(coeffs)),
    ):
        pairs = pairs_of(slots, lambda slot: slot ^ 2**j)
        level(pairs, load, lambda slot: slot, tables.at[j], weights.at[j], left, store)
    for step in range(0, size // 2, 32):
        rows = left.at[(step // 32) % 2]
        for i in range(32):
            for odd in range(2):
                slot = 2 * (step + i) + odd
                tile = turn(tables.at[3], slot, 0, split(coeffs[slot]))
                rows[16 * i : 16 * i + 16, 128 * odd : 128 * odd + 128] = tile
        product = jnp.dot(rows[...], wide[...], preferred_element_type=F32)
        for i in range(32):
            pair = step + i
            row = 32 * part[0] + pair
            cosine = trig[row : row + 1, 0:128]
            sine = trig[row : row + 1, 128:256]
            for half in range(2):
                real = product[16 * i : 16 * i + 8, 128 * half : 128 * half + 128]
                imag = product[16 * i + 8 : 16 * i + 16, 128 * half : 128 * half + 128]
                inputs = slice(8 * half, 8 * half + 8)
                points = slice(128 * pair, 128 * pair + 128)
                out[0, inputs, points] = real * cosine - imag * sine
                out[1, inputs, points] = real * sine + imag * cosine


def whole(shape):
    return pl.BlockSpec(shape, lambda i: (0,) * len(shape))


def levels(count, index):
    return pl.BlockSpec((count, 3, 64, 128), lambda i: (index, 0, 0, 0))


def scratch(slots, stages):
    return [
        pltpu.VMEM((slots, 16, 128), BF16),
        pltpu.VMEM((slots, 16, 128), BF16),
        pltpu.VMEM((stages, slots, 512), F32),
        pltpu.VMEM((2, 32 * PAIRS, 256), BF16),
        pltpu.VMEM((stages, 256, 128), BF16),
    ]


def call(kernel, name, in_specs, outs, scratch_shapes, **more):
    many = isinstance(outs, list)
    return pl.pallas_call(
        kernel,
        grid=(1,),
        in_specs=in_specs,
        out_specs=more.pop("out_specs", [whole(o.shape) for o in outs] if many else whole(outs.shape)),
        out_shape=outs,
        scratch_shapes=scratch_shapes,
        compiler_params=pltpu.CompilerParams(vmem_limit_bytes=40 * 1024 * 1024),
        name=name,
        **more,
    )


def shape_of(*shape, dtype=BF16):
    return jax.ShapeDtypeStruct(shape, dtype)


def shards(
    source_values,
    source_phase,
    leaf_interp,
    level_interp,
    level_phase,
    middle_interp,
    middle_phase,
    final_phase,
    final_interp,
    target_phase,
):
    phases = jnp.swapaxes(level_phase, 2, 3)
    middle = jnp.swapaxes(middle_phase, 1, 2)
    final = jnp.swapaxes(final_phase, 0, 1)
    interp_spec = whole((13, 2, 64, 64))
    matrix = whole((64, 64))
    angles = call(
        angle_kernel,
        "angles",
        [levels(2, 3), levels(2, 4), whole((2, 64, 128))],
        shape_of(128, 896),
        [],
    )(phases, phases, middle)
    angles = lax.all_to_all(
        angles.reshape(16, 8, 896), "tgt", split_axis=0, concat_axis=0, tiled=True
    ).reshape(128, 896)
    joined = []
    for part in E_PARTS:
        count = 8 * len(part)
        blocks = count + (5 if len(part) == 2 else 3)
        sent = call(
            functools.partial(source_kernel, part),
            "source_side",
            [whole((16, 8192)), whole((64, 128)), levels(6, 0), matrix, interp_spec],
            shape_of(8, blocks, 16, 128),
            scratch(8 * count, 3) + [pltpu.VMEM((64, 256), F32), pltpu.VMEM((256, 256), BF16)],
        )(source_values, source_phase.reshape(64, 128), phases, leaf_interp, level_interp)
        received = lax.all_to_all(sent, "src", split_axis=0, concat_axis=0, tiled=True)
        rows = pl.BlockSpec((8 * count, 896), lambda i, at=part[0]: (at, 0))
        joined.append(
            call(
                functools.partial(middle_kernel, part),
                "middle",
                [whole((8, blocks, 16, 128)), rows, interp_spec, matrix],
                shape_of(8 * count, 16, 128),
                scratch(8 * count, 8),
            )(received, angles, level_interp, middle_interp)
        )
    if len(E_PARTS) == 2:
        sent = call(
            join_kernel,
            "join",
            [whole((64, 16, 128)), whole((64, 16, 128)), whole((128, 896)), interp_spec],
            [shape_of(16, 4 * len(part), 16, 128) for part in D_PARTS],
            [
                pltpu.VMEM((128, 512), F32),
                pltpu.VMEM((2, 32 * PAIRS, 256), BF16),
                pltpu.VMEM((256, 128), BF16),
            ],
        )(*joined, angles, level_interp)
    else:
        sent = [joined[0].reshape(16, 8, 16, 128)]
    out = None
    for part, piece in zip(D_PARTS, sent):
        received = lax.all_to_all(piece, "tgt", split_axis=0, concat_axis=0, tiled=True)
        operands = [received, phases, phases, phases, phases, final, level_interp, final_interp]
        operands.append(target_phase.reshape(64, 128))
        specs = [whole(received.shape)] + [levels(1, n) for n in (9, 10, 11, 12)]
        specs += [whole((64, 128)), interp_spec, matrix, whole((64, 128))]
        more = {}
        if out is not None:
            operands.append(out)
            specs.append(pl.BlockSpec(memory_space=pl.ANY))
            more["input_output_aliases"] = {len(operands) - 1: 0}
        out = call(
            functools.partial(target_kernel, part),
            "target_side",
            specs,
            shape_of(2, 16, 8192, dtype=F32),
            scratch(64 * len(part), 4)
            + [pltpu.VMEM((64, 256), F32), pltpu.VMEM((256, 256), BF16)],
            out_specs=pl.BlockSpec(
                (2, 16, 4096 * len(part)), lambda i, at=part[0]: (0, 0, at)
            ),
            **more,
        )(*operands)
    return out


def solution(mesh):
    return jax.shard_map(
        shards,
        mesh=mesh,
        in_specs=(
            P(None, ("src", "tgt")),
            P(("src", "tgt")),
            P(),
            P(),
            P(None, None, ("src", "tgt"), None),
            P(),
            P(None, ("src", "tgt"), None),
            P(("src", "tgt"), None),
            P(),
            P(("src", "tgt")),
        ),
        out_specs=P(None, None, ("src", "tgt")),
        check_vma=False,
    )
```

```python
import functools

import functools

import jax
import jax.numpy as jnp
from jax import lax
from jax.experimental import pallas as pl
from jax.experimental.pallas import tpu as pltpu
from jax.sharding import PartitionSpec as P

F32 = jnp.float32
BF16 = jnp.bfloat16
PAIRS = 32
SIN_FIT = (3.14159258, -5.16770688, 2.55003138, -0.59804517, 0.07722012)
COS_FIT = (0.99999995, -4.93479286, 4.05841191, -1.33188014, 0.21969675)


def cos_sin(theta):
    turns = theta * F32(0.15915494309189535)
    turns = turns - jnp.round(turns)
    square = turns * turns
    sin_half = F32(SIN_FIT[4])
    cos_half = F32(COS_FIT[4])
    for k in (3, 2, 1, 0):
        sin_half = sin_half * square + F32(SIN_FIT[k])
        cos_half = cos_half * square + F32(COS_FIT[k])
    sin_half = sin_half * turns
    twice = sin_half + sin_half
    return 1.0 - twice * sin_half, twice * cos_half


def iota(shape, axis):
    return lax.broadcasted_iota(jnp.int32, shape, axis)


def xor_partner(values, stride, axis):
    size = values.shape[axis]
    bit = (iota(values.shape, axis) & stride) != 0
    return jnp.where(
        bit, pltpu.roll(values, stride, axis), pltpu.roll(values, size - stride, axis)
    )


def dot_last(left, right):
    return lax.dot_general(left, right, (((1,), (1,)), ((), ())), preferred_element_type=F32)


def permutation(size, row_of):
    rows = iota((size, size), 0)
    columns = iota((size, size), 1)
    return jnp.where(columns == row_of(rows), 1.0, 0.0).astype(BF16)


def lower(shape):
    return iota(shape, 1) < 64


def halves(matrix):
    matrix = matrix.astype(F32)
    doubled = jnp.concatenate([matrix, matrix], 1)
    zeros = jnp.zeros_like(doubled)
    low = lower(doubled.shape)
    return (
        jnp.where(low, doubled, zeros).astype(BF16),
        jnp.where(low, zeros, doubled).astype(BF16),
        zeros.astype(BF16),
    )


def put_weights(weights, matrices):
    for n, matrix in enumerate(matrices):
        low, high, _ = halves(matrix)
        weights[128 * n : 128 * n + 64, :] = low
        weights[128 * n + 64 : 128 * n + 128, :] = high


def put_trig(theta, table):
    low = lower(theta.shape)
    for at, value in zip((0, 128), cos_sin(theta)):
        turned = pltpu.roll(value, 64, 1)
        table[:, at : at + 128] = jnp.where(low, value, turned)
        table[:, at + 256 : at + 384] = jnp.where(low, turned, value)


def put_single_trig(theta, table):
    cosine, sine = cos_sin(theta)
    table[:, 0:128] = cosine
    table[:, 128:256] = sine


def turn(table, row, at, tile):
    real, imag = tile
    cosine = table[row : row + 1, at : at + 128]
    sine = table[row : row + 1, at + 128 : at + 256]
    turned = jnp.concatenate([real * cosine - imag * sine, real * sine + imag * cosine], 0)
    return turned.astype(BF16)


def split(tile):
    tile = tile.astype(F32)
    return tile[0:8], tile[8:16]


def level(pairs, load, row_of, table, weights, left, store):
    for step in range(0, len(pairs), PAIRS):
        rows = left.at[(step // PAIRS) % 2]
        chunk = pairs[step : step + PAIRS]
        slots = []
        for pair in chunk:
            tiles = [split(load(slot)) for slot in pair]
            for slot, own, other in zip(pair, tiles, tiles[::-1]):
                span = slice(16 * len(slots), 16 * len(slots) + 16)
                rows[span, 0:128] = turn(table, row_of(slot), 0, own)
                rows[span, 128:256] = turn(table, row_of(slot), 256, other)
                slots.append(slot)
        size = 16 * len(slots)
        product = jnp.dot(rows[:size, :], weights[...], preferred_element_type=F32).astype(BF16)
        for i, slot in enumerate(slots):
            store(slot, product[16 * i : 16 * i + 16])


def pairs_of(slots, partner):
    return [(slot, partner(slot)) for slot in slots if slot < partner(slot)]


def storer(ref):
    def store(slot, value):
        ref[slot] = value

    return store


def loader(ref):
    return lambda slot: ref[slot]


def angle_kernel(low_levels, high_levels, middle, out):
    me = lax.axis_index("src")
    pieces = [middle[0], middle[1]]
    for ref, n in ((low_levels, 0), (low_levels, 1), (high_levels, 0), (high_levels, 1)):
        pieces += [ref[n, 0], ref[n, 1]]
    pieces += [low_levels[0, 2], low_levels[1, 2], high_levels[0, 2], high_levels[0, 2]]
    stacked = jnp.concatenate([piece.astype(BF16) for piece in pieces], 0)
    perm = permutation(128, lambda rows: ((rows & 7) ^ me) * 16 + (rows >> 3))
    out[...] = dot_last(perm, stacked).astype(BF16)


def source_kernel(
    part, values, phase, phases, leaf, interp, *rest
):
    outs = rest[:8]
    out, coeffs, spare, tables, left, weights, trig, wide = rest[8:]
    count = 8 * len(part)

    def rows_here(value):
        if len(part) == 2:
            return value
        width = value.shape[1]
        return value.reshape(8, 2, 8, width)[:, part[0]].reshape(64, width)

    pieces = [phases[n, q] for n in (3, 4, 5) for q in (0, 1)]
    pieces += [phases[n, 2] for n in (2, 3, 4, 5)]
    stacked = jnp.concatenate([piece.astype(BF16) for piece in pieces], 0)
    sent = rows_here(dot_last(permutation(128, lambda rows: rows), stacked))
    for e in range(8):
        here = sent[count * e : count * e + count]
        if len(part) == 2:
            for p in range(5):
                out[e, count + p] = here[:, 128 * p : 128 * p + 128].astype(BF16)
        else:
            for p in range(3):
                first = here[:, 256 * p : 256 * p + 128]
                second = here[:, 256 * p + 128 : 256 * p + 256] if p < 2 else first
                out[e, count + p] = jnp.concatenate([first, second], 0).astype(BF16)
    for n in range(3):
        own, other = phases[n, 0], phases[n, 1]
        if n:
            own = own + phases[n - 1, 2]
            other = other + xor_partner(phases[n - 1, 2], 2**n, 1)
        put_trig(rows_here(jnp.transpose(jnp.concatenate([own, other], 0))), tables.at[n])
        put_weights(weights.at[n], [interp[n, 0], interp[n, 1]])
    put_single_trig(phase[...], trig)
    low, high, zeros = halves(leaf[...])
    for n, first, second in ((0, low, zeros), (1, zeros, low), (2, high, zeros), (3, zeros, high)):
        wide[64 * n : 64 * n + 64, 0:128] = first
        wide[64 * n : 64 * n + 64, 128:256] = second
    leaf_pairs = [pair for pair in range(64) if (pair >> 2) & 1 in part]
    place = lambda slot: (slot >> 4) * count + (slot & (count - 1))
    for step in range(0, len(leaf_pairs), 32):
        rows = left.at[(step // 32) % 2]
        chunk = leaf_pairs[step : step + 32]
        for i, pair in enumerate(chunk):
            cosine = trig[pair : pair + 1, 0:128]
            sine = -trig[pair : pair + 1, 128:256]
            for half in range(2):
                block = values[8 * half : 8 * half + 8, 128 * pair : 128 * pair + 128]
                tile = jnp.concatenate([block * cosine, block * sine], 0).astype(BF16)
                rows[16 * i : 16 * i + 16, 128 * half : 128 * half + 128] = tile
        product = jnp.dot(rows[:512, :], wide[...], preferred_element_type=F32).astype(BF16)
        for i, pair in enumerate(chunk):
            coeffs[place(2 * pair)] = product[16 * i : 16 * i + 16, 0:128]
            coeffs[place(2 * pair + 1)] = product[16 * i : 16 * i + 16, 128:256]

    def send(slot, value):
        out[slot // count, slot % count] = value

    slots = range(8 * count)
    for n, load, store in (
        (0, loader(coeffs), storer(spare)),
        (1, loader(spare), storer(coeffs)),
        (2, loader(coeffs), send),
    ):
        pairs = pairs_of(slots, lambda slot: slot ^ 2**n)
        level(pairs, load, lambda slot: slot, tables.at[n], weights.at[n], left, store)
    me = lax.axis_index("src")
    for k in range(8):
        outs[k][...] = out[me ^ k]


def both(value, half):
    low = lower(value.shape)
    turned = pltpu.roll(value, 64, 1)
    return jnp.where(low, value, turned) if half == 0 else jnp.where(low, turned, value)


def with_partner(value, stride):
    return jnp.where(lower(value.shape), value, xor_partner(value, stride, 0))


def late_table_kernel(angles, interp, middle_interp, tables, weights):
    late = lambda p: angles[:, 128 * p : 128 * p + 128].astype(F32)
    pending = both(late(0), 1)
    for j in range(4):
        put_trig(late(1 + j) + with_partner(pending, 8 * 2**j), tables.at[j])
        if j < 3:
            pending = both(late(5 + j // 2), j % 2)
    for j in range(3):
        put_weights(weights.at[j], [interp[3 + j, 0], interp[3 + j, 1]])
    put_weights(weights.at[3], [middle_interp[...], middle_interp[...]])
    for j in range(4):
        put_weights(weights.at[4 + j], [interp[6 + j, 0], interp[6 + j, 1]])


def middle_kernel(
    part, *refs
):
    received = refs[:8]
    angles, late_tables, weights, out, coeffs, spare, tables, left = refs[8:]
    count = 8 * len(part)
    size = 8 * count
    early = []
    for p in range(5):
        if len(part) == 2:
            tiles = [received[d][count + p].astype(F32) for d in range(8)]
        else:
            at = 8 * (p % 2)
            tiles = [received[d][count + p // 2].astype(F32)[at : at + 8] for d in range(8)]
        early.append(jnp.concatenate(tiles, 0))
    late = lambda p: angles[:, 128 * p : 128 * p + 128].astype(F32)
    pending = both(early[3], 0)
    for j in range(3):
        put_trig(early[j] + with_partner(pending, count * 2**j), tables.at[j])
        pending = both(early[3 + (j + 1) // 2], (j + 1) % 2)
    perm = permutation(size, lambda rows: (rows & 7) * count + (rows >> 3))
    pending = jnp.dot(perm, pending.astype(BF16), preferred_element_type=F32)
    put_single_trig(pending + both(late(0), 0), tables.at[3])

    def arrived(slot):
        return received[slot & 7][slot >> 3]

    def turned_row(slot):
        return (slot & 7) * count + (slot >> 3)

    slots = range(size)
    stores = [storer(coeffs), storer(spare)]
    loads = [loader(coeffs), loader(spare)]
    for j in range(3):
        level(
            pairs_of(slots, lambda slot: slot ^ 2**j),
            arrived if j == 0 else loads[(j + 1) % 2],
            turned_row,
            tables.at[j],
            weights.at[j],
            left,
            stores[j % 2],
        )
    for step in range(0, size, 32):
        rows = left.at[(step // 32) % 2]
        for i in range(32):
            tile = split(coeffs[step + i])
            rows[16 * i : 16 * i + 16, 0:128] = turn(tables.at[3], step + i, 0, tile)
        product = jnp.dot(
            rows[:512, 0:128], weights[3, 0:128, :], preferred_element_type=F32
        ).astype(BF16)
        for i in range(32):
            spare[step + i] = product[16 * i : 16 * i + 16]
    last = len(part) + 1
    for j in range(last + 1):
        level(
            pairs_of(slots, lambda slot: slot ^ 8 * 2**j),
            loads[(j + 1) % 2],
            lambda slot: slot,
            late_tables.at[j],
            weights.at[4 + j],
            left,
            storer(out) if j == last else stores[j % 2],
        )


def target_table_kernel(phases, final, interp, phase, tables, weights, trig):
    pending = phases[9, 2]
    for j in range(3):
        own = phases[10 + j, 0] + pending
        other = phases[10 + j, 1] + xor_partner(pending, 2**j, 1)
        put_trig(jnp.transpose(jnp.concatenate([own, other], 0)), tables.at[j])
        put_weights(weights.at[j], [interp[10 + j, 0], interp[10 + j, 1]])
        pending = phases[10 + j, 2]
    pending = final[...] + pending
    put_single_trig(jnp.transpose(jnp.concatenate([pending, pending], 0)), tables.at[3])
    put_single_trig(phase[...], trig)


def target_kernel(
    received, tables, weights, trig, final_interp, result, coeffs, spare, left, wide, out, sems
):
    me = lax.axis_index("src")
    low, high, zeros = halves(final_interp[...])
    for n, first, second in ((0, low, zeros), (1, zeros, low), (2, high, zeros), (3, zeros, high)):
        wide[64 * n : 64 * n + 64, 0:128] = first
        wide[64 * n : 64 * n + 64, 128:256] = second
    size = 128
    copies = []
    slots = range(size)
    for j, load, store in (
        (0, lambda slot: received[slot & 15, (slot >> 4) ^ me], storer(coeffs)),
        (1, loader(coeffs), storer(spare)),
        (2, loader(spare), storer(coeffs)),
    ):
        pairs = pairs_of(slots, lambda slot: slot ^ 2**j)
        level(pairs, load, lambda slot: slot, tables.at[j], weights.at[j], left, store)
    for step in range(0, size // 2, 16):
        rows = left.at[(step // 16) % 2]
        for i in range(16):
            for odd in range(2):
                slot = 2 * (step + i) + odd
                tile = turn(tables.at[3], slot, 0, split(coeffs[slot]))
                rows[16 * i : 16 * i + 16, 128 * odd : 128 * odd + 128] = tile
        product = jnp.dot(rows[:256, :], wide[...], preferred_element_type=F32)
        for i in range(16):
            pair = step + i
            row = pair
            cosine = trig[row : row + 1, 0:128]
            sine = trig[row : row + 1, 128:256]
            for half in range(2):
                real = product[16 * i : 16 * i + 8, 128 * half : 128 * half + 128]
                imag = product[16 * i + 8 : 16 * i + 16, 128 * half : 128 * half + 128]
                inputs = slice(8 * half, 8 * half + 8)
                points = slice(128 * pair, 128 * pair + 128)
                out[0, inputs, points] = real * cosine - imag * sine
                out[1, inputs, points] = real * sine + imag * cosine
        points = slice(128 * step, 128 * step + 2048)
        copies.append(
            pltpu.make_async_copy(
                out.at[:, :, points], result.at[:, :, points], sems.at[step // 16]
            )
        )
        copies[-1].start()
    for copy in copies:
        copy.wait()


def whole(_):
    return pl.BlockSpec(memory_space=pltpu.VMEM)


def levels(count, index):
    return pl.BlockSpec((count, 3, 64, 128), lambda i: (index, 0, 0, 0))


def call(kernel, name, in_specs, outs, scratch_shapes, **more):
    many = isinstance(outs, list)
    return pl.pallas_call(
        kernel,
        in_specs=in_specs,
        out_specs=more.pop("out_specs", [whole(o.shape) for o in outs] if many else whole(outs.shape)),
        out_shape=outs,
        scratch_shapes=scratch_shapes,
        compiler_params=pltpu.CompilerParams(vmem_limit_bytes=more.pop("room", 24) * 1024 * 1024),
        name=name,
        **more,
    )


def shape_of(*shape, dtype=BF16):
    return jax.ShapeDtypeStruct(shape, dtype)


def shards(
    source_values,
    source_phase,
    leaf_interp,
    level_interp,
    level_phase,
    middle_interp,
    middle_phase,
    final_phase,
    final_interp,
    target_phase,
):
    phases = jnp.swapaxes(level_phase, 2, 3)
    middle = jnp.swapaxes(middle_phase, 1, 2)
    final = jnp.swapaxes(final_phase, 0, 1)
    interp_spec = whole((13, 2, 64, 64))
    matrix = whole((64, 64))
    angles = call(
        angle_kernel,
        "angles",
        [levels(2, 3), levels(2, 4), pl.BlockSpec((2, 64, 128), lambda i: (0, 0, 0))],
        shape_of(128, 896),
        [],
        grid=(1,),
        out_specs=pl.BlockSpec((128, 896), lambda i: (0, 0)),
        room=60,
    )(phases, phases, middle)
    angles = lax.all_to_all(
        angles.reshape(16, 8, 896), "tgt", split_axis=0, concat_axis=0, tiled=True
    ).reshape(128, 896)
    late_tables, weights = call(
        late_table_kernel,
        "late_tables",
        [whole(None)] * 3,
        [shape_of(4, 128, 512, dtype=F32), shape_of(8, 256, 128)],
        [],
    )(angles, level_interp, middle_interp)
    target_tables = call(
        target_table_kernel,
        "target_tables",
        [whole(None)] * 4,
        [
            shape_of(4, 128, 512, dtype=F32),
            shape_of(3, 256, 128),
            shape_of(64, 256, dtype=F32),
        ],
        [],
    )(phases, final, level_interp, target_phase.reshape(64, 128))
    tiles = pltpu.VMEM((128, 16, 128), BF16)
    left = pltpu.VMEM((2, 32 * PAIRS, 256), BF16)
    part = (0, 1)
    sent = call(
        functools.partial(source_kernel, part),
        "source_side",
        [whole(None)] * 5,
        [shape_of(21, 16, 128)] * 8,
        [pltpu.VMEM((8, 21, 16, 128), BF16), tiles, tiles]
        + [pltpu.VMEM((3, 128, 512), F32), left, pltpu.VMEM((3, 256, 128), BF16)]
        + [pltpu.VMEM((64, 256), F32), pltpu.VMEM((256, 256), BF16)],
    )(source_values, source_phase.reshape(64, 128), phases, leaf_interp, level_interp)
    received = [
        lax.ppermute(piece, "src", [(i, i ^ k) for i in range(8)]) if k else piece
        for k, piece in enumerate(sent)
    ]
    sent = call(
        functools.partial(middle_kernel, part),
        "middle",
        [whole(None)] * 11,
        shape_of(128, 16, 128),
        [tiles, tiles, pltpu.VMEM((4, 128, 512), F32), left],
    )(*received, angles, late_tables, weights)
    received = lax.all_to_all(
        sent.reshape(16, 8, 16, 128), "tgt", split_axis=0, concat_axis=0, tiled=True
    )
    return call(
        target_kernel,
        "target_side",
        [whole(None)] * 5,
        shape_of(2, 16, 8192, dtype=F32),
        [tiles, tiles, left, pltpu.VMEM((256, 256), BF16)]
        + [pltpu.VMEM((2, 16, 8192), F32), pltpu.SemaphoreType.DMA((4,))],
        out_specs=pl.BlockSpec(memory_space=pl.ANY),
    )(received, *target_tables, final_interp)


def solution(mesh):
    return jax.shard_map(
        shards,
        mesh=mesh,
        in_specs=(
            P(None, ("src", "tgt")),
            P(("src", "tgt")),
            P(),
            P(),
            P(None, None, ("src", "tgt"), None),
            P(),
            P(None, ("src", "tgt"), None),
            P(("src", "tgt"), None),
            P(),
            P(("src", "tgt")),
        ),
        out_specs=P(None, None, ("src", "tgt")),
        check_vma=False,
    )
```

```python
import functools

import functools

import jax
import jax.numpy as jnp
from jax import lax
from jax.experimental import pallas as pl
from jax.experimental.pallas import tpu as pltpu
from jax.sharding import PartitionSpec as P

F32 = jnp.float32
BF16 = jnp.bfloat16
PAIRS = 32
SIN_FIT = (3.14159258, -5.16770688, 2.55003138, -0.59804517, 0.07722012)
COS_FIT = (0.99999995, -4.93479286, 4.05841191, -1.33188014, 0.21969675)


def cos_sin(theta):
    turns = theta * F32(0.15915494309189535)
    turns = turns - jnp.round(turns)
    square = turns * turns
    sin_half = F32(SIN_FIT[4])
    cos_half = F32(COS_FIT[4])
    for k in (3, 2, 1, 0):
        sin_half = sin_half * square + F32(SIN_FIT[k])
        cos_half = cos_half * square + F32(COS_FIT[k])
    sin_half = sin_half * turns
    twice = sin_half + sin_half
    return 1.0 - twice * sin_half, twice * cos_half


def iota(shape, axis):
    return lax.broadcasted_iota(jnp.int32, shape, axis)


def xor_partner(values, stride, axis):
    size = values.shape[axis]
    bit = (iota(values.shape, axis) & stride) != 0
    return jnp.where(
        bit, pltpu.roll(values, stride, axis), pltpu.roll(values, size - stride, axis)
    )


def dot_last(left, right):
    return lax.dot_general(left, right, (((1,), (1,)), ((), ())), preferred_element_type=F32)


def permutation(size, row_of):
    rows = iota((size, size), 0)
    columns = iota((size, size), 1)
    return jnp.where(columns == row_of(rows), 1.0, 0.0).astype(BF16)


def lower(shape):
    return iota(shape, 1) < 64


def halves(matrix):
    matrix = matrix.astype(F32)
    doubled = jnp.concatenate([matrix, matrix], 1)
    zeros = jnp.zeros_like(doubled)
    low = lower(doubled.shape)
    return (
        jnp.where(low, doubled, zeros).astype(BF16),
        jnp.where(low, zeros, doubled).astype(BF16),
        zeros.astype(BF16),
    )


def put_weights(weights, matrices):
    for n, matrix in enumerate(matrices):
        low, high, _ = halves(matrix)
        weights[128 * n : 128 * n + 64, :] = low
        weights[128 * n + 64 : 128 * n + 128, :] = high


def put_trig(theta, table):
    low = lower(theta.shape)
    for at, value in zip((0, 128), cos_sin(theta)):
        turned = pltpu.roll(value, 64, 1)
        table[:, at : at + 128] = jnp.where(low, value, turned)
        table[:, at + 256 : at + 384] = jnp.where(low, turned, value)


def put_single_trig(theta, table):
    cosine, sine = cos_sin(theta)
    table[:, 0:128] = cosine
    table[:, 128:256] = sine


def turn(table, row, at, tile):
    real, imag = tile
    cosine = table[row : row + 1, at : at + 128]
    sine = table[row : row + 1, at + 128 : at + 256]
    turned = jnp.concatenate([real * cosine - imag * sine, real * sine + imag * cosine], 0)
    return turned.astype(BF16)


def split(tile):
    tile = tile.astype(F32)
    return tile[0:8], tile[8:16]


def level(pairs, load, row_of, table, weights, left, store):
    for step in range(0, len(pairs), PAIRS):
        rows = left.at[(step // PAIRS) % 2]
        chunk = pairs[step : step + PAIRS]
        slots = []
        for pair in chunk:
            tiles = [split(load(slot)) for slot in pair]
            for slot, own, other in zip(pair, tiles, tiles[::-1]):
                span = slice(16 * len(slots), 16 * len(slots) + 16)
                rows[span, 0:128] = turn(table, row_of(slot), 0, own)
                rows[span, 128:256] = turn(table, row_of(slot), 256, other)
                slots.append(slot)
        size = 16 * len(slots)
        product = jnp.dot(rows[:size, :], weights[...], preferred_element_type=F32).astype(BF16)
        for i, slot in enumerate(slots):
            store(slot, product[16 * i : 16 * i + 16])


def pairs_of(slots, partner):
    return [(slot, partner(slot)) for slot in slots if slot < partner(slot)]


def storer(ref):
    def store(slot, value):
        ref[slot] = value

    return store


def loader(ref):
    return lambda slot: ref[slot]


def angle_kernel(low_levels, high_levels, middle, out):
    me = lax.axis_index("src")
    pieces = [middle[0], middle[1]]
    for ref, n in ((low_levels, 0), (low_levels, 1), (high_levels, 0), (high_levels, 1)):
        pieces += [ref[n, 0], ref[n, 1]]
    pieces += [low_levels[0, 2], low_levels[1, 2], high_levels[0, 2], high_levels[0, 2]]
    stacked = jnp.concatenate([piece.astype(BF16) for piece in pieces], 0)
    perm = permutation(128, lambda rows: ((rows & 7) ^ me) * 16 + (rows >> 3))
    out[...] = dot_last(perm, stacked).astype(BF16)


def source_kernel(
    part, values, phase, phases, leaf, interp, *rest
):
    outs = rest[:8]
    out, coeffs, spare, tables, left, weights, trig, wide = rest[8:]
    count = 8 * len(part)

    def rows_here(value):
        if len(part) == 2:
            return value
        width = value.shape[1]
        return value.reshape(8, 2, 8, width)[:, part[0]].reshape(64, width)

    pieces = [phases[n, q] for n in (3, 4, 5) for q in (0, 1)]
    pieces += [phases[n, 2] for n in (2, 3, 4, 5)]
    stacked = jnp.concatenate([piece.astype(BF16) for piece in pieces], 0)
    sent = rows_here(dot_last(permutation(128, lambda rows: rows), stacked))
    for e in range(8):
        here = sent[count * e : count * e + count]
        if len(part) == 2:
            for p in range(5):
                out[e, count + p] = here[:, 128 * p : 128 * p + 128].astype(BF16)
        else:
            for p in range(3):
                first = here[:, 256 * p : 256 * p + 128]
                second = here[:, 256 * p + 128 : 256 * p + 256] if p < 2 else first
                out[e, count + p] = jnp.concatenate([first, second], 0).astype(BF16)
    for n in range(3):
        own, other = phases[n, 0], phases[n, 1]
        if n:
            own = own + phases[n - 1, 2]
            other = other + xor_partner(phases[n - 1, 2], 2**n, 1)
        put_trig(rows_here(jnp.transpose(jnp.concatenate([own, other], 0))), tables.at[n])
        put_weights(weights.at[n], [interp[n, 0], interp[n, 1]])
    put_single_trig(phase[...], trig)
    low, high, zeros = halves(leaf[...])
    for n, first, second in ((0, low, zeros), (1, zeros, low), (2, high, zeros), (3, zeros, high)):
        wide[64 * n : 64 * n + 64, 0:128] = first
        wide[64 * n : 64 * n + 64, 128:256] = second
    leaf_pairs = [pair for pair in range(64) if (pair >> 2) & 1 in part]
    place = lambda slot: (slot >> 4) * count + (slot & (count - 1))
    for step in range(0, len(leaf_pairs), 32):
        rows = left.at[(step // 32) % 2]
        chunk = leaf_pairs[step : step + 32]
        for i, pair in enumerate(chunk):
            cosine = trig[pair : pair + 1, 0:128]
            sine = -trig[pair : pair + 1, 128:256]
            for half in range(2):
                block = values[8 * half : 8 * half + 8, 128 * pair : 128 * pair + 128]
                tile = jnp.concatenate([block * cosine, block * sine], 0).astype(BF16)
                rows[16 * i : 16 * i + 16, 128 * half : 128 * half + 128] = tile
        product = jnp.dot(rows[:512, :], wide[...], preferred_element_type=F32).astype(BF16)
        for i, pair in enumerate(chunk):
            coeffs[place(2 * pair)] = product[16 * i : 16 * i + 16, 0:128]
            coeffs[place(2 * pair + 1)] = product[16 * i : 16 * i + 16, 128:256]

    def send(slot, value):
        out[slot // count, slot % count] = value

    slots = range(8 * count)
    for n, load, store in (
        (0, loader(coeffs), storer(spare)),
        (1, loader(spare), storer(coeffs)),
        (2, loader(coeffs), send),
    ):
        pairs = pairs_of(slots, lambda slot: slot ^ 2**n)
        level(pairs, load, lambda slot: slot, tables.at[n], weights.at[n], left, store)
    me = lax.axis_index("src")
    for k in range(8):
        outs[k][...] = out[me ^ k]


def both(value, half):
    low = lower(value.shape)
    turned = pltpu.roll(value, 64, 1)
    return jnp.where(low, value, turned) if half == 0 else jnp.where(low, turned, value)


def with_partner(value, stride):
    return jnp.where(lower(value.shape), value, xor_partner(value, stride, 0))


def late_table_kernel(angles, interp, middle_interp, tables, weights):
    late = lambda p: angles[:, 128 * p : 128 * p + 128].astype(F32)
    pending = both(late(0), 1)
    for j in range(4):
        put_trig(late(1 + j) + with_partner(pending, 8 * 2**j), tables.at[j])
        if j < 3:
            pending = both(late(5 + j // 2), j % 2)
    for j in range(3):
        put_weights(weights.at[j], [interp[3 + j, 0], interp[3 + j, 1]])
    put_weights(weights.at[3], [middle_interp[...], middle_interp[...]])
    for j in range(4):
        put_weights(weights.at[4 + j], [interp[6 + j, 0], interp[6 + j, 1]])


def near_kernel(*refs):
    received = refs[:4]
    interp, out, coeffs, tables, left, weights = refs[4:]
    early = [
        jnp.concatenate([received[d][16 + p].astype(F32) for d in range(4)], 0) for p in (0, 1, 3)
    ]
    for j in range(2):
        theta = early[j] + with_partner(both(early[2], j), 16 * 2**j)
        put_trig(theta, tables.at[j])
        put_weights(weights.at[j], [interp[3 + j, 0], interp[3 + j, 1]])

    def send(slot, value):
        out[slot >> 4, slot & 15] = value

    for j, load, store in (
        (0, lambda slot: received[slot >> 4][slot & 15], storer(coeffs)),
        (1, loader(coeffs), send),
    ):
        pairs = pairs_of(range(64), lambda slot: slot ^ 16 * 2**j)
        level(pairs, load, lambda slot: slot, tables.at[j], weights.at[j], left, store)


def middle_kernel(
    part, *refs
):
    received = refs[:8]
    near, angles, late_tables, weights, out, coeffs, spare, tables, left = refs[8:]
    count = 8 * len(part)
    size = 8 * count
    early = []
    for p in range(5):
        if len(part) == 2:
            tiles = [received[d][count + p].astype(F32) for d in range(8)]
        else:
            at = 8 * (p % 2)
            tiles = [received[d][count + p // 2].astype(F32)[at : at + 8] for d in range(8)]
        early.append(jnp.concatenate(tiles, 0))
    late = lambda p: angles[:, 128 * p : 128 * p + 128].astype(F32)
    pending = both(early[3], 0)
    for j in range(3):
        theta = early[j] + with_partner(pending, count * 2**j)
        if j < 2:
            put_trig(theta[64:128], tables.at[j, 64:128])
        else:
            put_trig(theta, tables.at[j])
        pending = both(early[3 + (j + 1) // 2], (j + 1) % 2)
    perm = permutation(size, lambda rows: (rows & 7) * count + (rows >> 3))
    pending = jnp.dot(perm, pending.astype(BF16), preferred_element_type=F32)
    put_single_trig(pending + both(late(0), 0), tables.at[3])

    def arrived(slot):
        return received[slot & 7][slot >> 3]

    def turned_row(slot):
        return (slot & 7) * count + (slot >> 3)

    slots = range(size)
    stores = [storer(coeffs), storer(spare)]
    loads = [loader(coeffs), loader(spare)]
    far = [slot for slot in slots if slot & 4]

    def halfway(slot):
        return spare[slot] if slot & 4 else near[slot & 7, slot >> 3]

    for j, load in enumerate((arrived, loads[0], halfway)):
        level(
            pairs_of(far if j < 2 else slots, lambda slot: slot ^ 2**j),
            load,
            turned_row,
            tables.at[j],
            weights.at[j],
            left,
            stores[j % 2],
        )
    for step in range(0, size, 32):
        rows = left.at[(step // 32) % 2]
        for i in range(32):
            tile = split(coeffs[step + i])
            rows[16 * i : 16 * i + 16, 0:128] = turn(tables.at[3], step + i, 0, tile)
        product = jnp.dot(
            rows[:512, 0:128], weights[3, 0:128, :], preferred_element_type=F32
        ).astype(BF16)
        for i in range(32):
            spare[step + i] = product[16 * i : 16 * i + 16]
    last = len(part) + 1
    for j in range(last + 1):
        level(
            pairs_of(slots, lambda slot: slot ^ 8 * 2**j),
            loads[(j + 1) % 2],
            lambda slot: slot,
            late_tables.at[j],
            weights.at[4 + j],
            left,
            storer(out) if j == last else stores[j % 2],
        )


def target_table_kernel(phases, final, interp, phase, tables, weights, trig):
    pending = phases[9, 2]
    for j in range(3):
        own = phases[10 + j, 0] + pending
        other = phases[10 + j, 1] + xor_partner(pending, 2**j, 1)
        put_trig(jnp.transpose(jnp.concatenate([own, other], 0)), tables.at[j])
        put_weights(weights.at[j], [interp[10 + j, 0], interp[10 + j, 1]])
        pending = phases[10 + j, 2]
    pending = final[...] + pending
    put_single_trig(jnp.transpose(jnp.concatenate([pending, pending], 0)), tables.at[3])
    put_single_trig(phase[...], trig)


def target_kernel(
    received, tables, weights, trig, final_interp, result, coeffs, spare, left, wide, out, sems
):
    me = lax.axis_index("src")
    low, high, zeros = halves(final_interp[...])
    for n, first, second in ((0, low, zeros), (1, zeros, low), (2, high, zeros), (3, zeros, high)):
        wide[64 * n : 64 * n + 64, 0:128] = first
        wide[64 * n : 64 * n + 64, 128:256] = second
    size = 128
    copies = []
    slots = range(size)
    for j, load, store in (
        (0, lambda slot: received[slot & 15, (slot >> 4) ^ me], storer(coeffs)),
        (1, loader(coeffs), storer(spare)),
        (2, loader(spare), storer(coeffs)),
    ):
        pairs = pairs_of(slots, lambda slot: slot ^ 2**j)
        level(pairs, load, lambda slot: slot, tables.at[j], weights.at[j], left, store)
    for step in range(0, size // 2, 16):
        rows = left.at[(step // 16) % 2]
        for i in range(16):
            for odd in range(2):
                slot = 2 * (step + i) + odd
                tile = turn(tables.at[3], slot, 0, split(coeffs[slot]))
                rows[16 * i : 16 * i + 16, 128 * odd : 128 * odd + 128] = tile
        product = jnp.dot(rows[:256, :], wide[...], preferred_element_type=F32)
        for i in range(16):
            pair = step + i
            row = pair
            cosine = trig[row : row + 1, 0:128]
            sine = trig[row : row + 1, 128:256]
            for half in range(2):
                real = product[16 * i : 16 * i + 8, 128 * half : 128 * half + 128]
                imag = product[16 * i + 8 : 16 * i + 16, 128 * half : 128 * half + 128]
                inputs = slice(8 * half, 8 * half + 8)
                points = slice(128 * pair, 128 * pair + 128)
                out[0, inputs, points] = real * cosine - imag * sine
                out[1, inputs, points] = real * sine + imag * cosine
        points = slice(128 * step, 128 * step + 2048)
        copies.append(
            pltpu.make_async_copy(
                out.at[:, :, points], result.at[:, :, points], sems.at[step // 16]
            )
        )
        copies[-1].start()
    for copy in copies:
        copy.wait()


def whole(_):
    return pl.BlockSpec(memory_space=pltpu.VMEM)


def levels(count, index):
    return pl.BlockSpec((count, 3, 64, 128), lambda i: (index, 0, 0, 0))


def call(kernel, name, in_specs, outs, scratch_shapes, **more):
    many = isinstance(outs, list)
    return pl.pallas_call(
        kernel,
        in_specs=in_specs,
        out_specs=more.pop("out_specs", [whole(o.shape) for o in outs] if many else whole(outs.shape)),
        out_shape=outs,
        scratch_shapes=scratch_shapes,
        compiler_params=pltpu.CompilerParams(vmem_limit_bytes=more.pop("room", 24) * 1024 * 1024),
        name=name,
        **more,
    )


def shape_of(*shape, dtype=BF16):
    return jax.ShapeDtypeStruct(shape, dtype)


def shards(
    source_values,
    source_phase,
    leaf_interp,
    level_interp,
    level_phase,
    middle_interp,
    middle_phase,
    final_phase,
    final_interp,
    target_phase,
):
    phases = jnp.swapaxes(level_phase, 2, 3)
    middle = jnp.swapaxes(middle_phase, 1, 2)
    final = jnp.swapaxes(final_phase, 0, 1)
    interp_spec = whole((13, 2, 64, 64))
    matrix = whole((64, 64))
    angles = call(
        angle_kernel,
        "angles",
        [levels(2, 3), levels(2, 4), pl.BlockSpec((2, 64, 128), lambda i: (0, 0, 0))],
        shape_of(128, 896),
        [],
        grid=(1,),
        out_specs=pl.BlockSpec((128, 896), lambda i: (0, 0)),
        room=60,
    )(phases, phases, middle)
    angles = lax.all_to_all(
        angles.reshape(16, 8, 896), "tgt", split_axis=0, concat_axis=0, tiled=True
    ).reshape(128, 896)
    late_tables, weights = call(
        late_table_kernel,
        "late_tables",
        [whole(None)] * 3,
        [shape_of(4, 128, 512, dtype=F32), shape_of(8, 256, 128)],
        [],
    )(angles, level_interp, middle_interp)
    target_tables = call(
        target_table_kernel,
        "target_tables",
        [whole(None)] * 4,
        [
            shape_of(4, 128, 512, dtype=F32),
            shape_of(3, 256, 128),
            shape_of(64, 256, dtype=F32),
        ],
        [],
    )(phases, final, level_interp, target_phase.reshape(64, 128))
    tiles = pltpu.VMEM((128, 16, 128), BF16)
    left = pltpu.VMEM((2, 32 * PAIRS, 256), BF16)
    part = (0, 1)
    sent = call(
        functools.partial(source_kernel, part),
        "source_side",
        [whole(None)] * 5,
        [shape_of(21, 16, 128)] * 8,
        [pltpu.VMEM((8, 21, 16, 128), BF16), tiles, tiles]
        + [pltpu.VMEM((3, 128, 512), F32), left, pltpu.VMEM((3, 256, 128), BF16)]
        + [pltpu.VMEM((64, 256), F32), pltpu.VMEM((256, 256), BF16)],
    )(source_values, source_phase.reshape(64, 128), phases, leaf_interp, level_interp)
    received = [
        lax.ppermute(piece, "src", [(i, i ^ k) for i in range(8)]) if k else piece
        for k, piece in enumerate(sent)
    ]
    near = call(
        near_kernel,
        "near",
        [whole(None)] * 5,
        shape_of(4, 16, 16, 128),
        [pltpu.VMEM((64, 16, 128), BF16), pltpu.VMEM((2, 64, 512), F32), left]
        + [pltpu.VMEM((2, 256, 128), BF16)],
    )(*received[:4], level_interp)
    sent = call(
        functools.partial(middle_kernel, part),
        "middle",
        [whole(None)] * 12,
        shape_of(128, 16, 128),
        [tiles, tiles, pltpu.VMEM((4, 128, 512), F32), left],
    )(*received, near, angles, late_tables, weights)
    received = lax.all_to_all(
        sent.reshape(16, 8, 16, 128), "tgt", split_axis=0, concat_axis=0, tiled=True
    )
    return call(
        target_kernel,
        "target_side",
        [whole(None)] * 5,
        shape_of(2, 16, 8192, dtype=F32),
        [tiles, tiles, left, pltpu.VMEM((256, 256), BF16)]
        + [pltpu.VMEM((2, 16, 8192), F32), pltpu.SemaphoreType.DMA((4,))],
        out_specs=pl.BlockSpec(memory_space=pl.ANY),
    )(received, *target_tables, final_interp)


def solution(mesh):
    return jax.shard_map(
        shards,
        mesh=mesh,
        in_specs=(
            P(None, ("src", "tgt")),
            P(("src", "tgt")),
            P(),
            P(),
            P(None, None, ("src", "tgt"), None),
            P(),
            P(None, ("src", "tgt"), None),
            P(("src", "tgt"), None),
            P(),
            P(("src", "tgt")),
        ),
        out_specs=P(None, None, ("src", "tgt")),
        check_vma=False,
    )
```
